32 devices in a mesh: req: 8 (over z, x), tp: 4 (over y, core).
Axes of the slice: x: 2, y: 2, z: 4, core: 2. Of those that a mesh axis runs over, the one named last changes fastest.
Arguments:
- layer_in: bfloat16 [4, 64, 2880], P(None, 'req'), may hold values from -3 to 3
- query_in: bfloat16 [4, 64, 2048], P(None, 'req', 'tp'), may hold values from -6 to 6
- unrotated_key: bfloat16 [4, 64, 512], P(None, 'req', 'tp'), may hold values from -6 to 6
- incoming_value: bfloat16 [4, 64, 512], P(None, 'req', 'tp'), may hold values from -12 to 12
- rotated_prompt_keys: bfloat16 [64, 256, 512], P('req', None, 'tp'), may hold values from -270 to 270
- prompt_value_rows: bfloat16 [64, 256, 512], P('req', None, 'tp'), may hold values from -6 to 6
- generated_key_rows: bfloat16 [64, 64, 512], P('req', None, 'tp'), may hold values from -9 to 9
- generated_value_rows: bfloat16 [64, 64, 512], P('req', None, 'tp'), may hold values from -12 to 12
- lengths: int32 [8], replicated, may hold values from 128 to 2048, as said below
- parents: int32 [4, 8, 8], replicated, may hold values from 0 to 7
- routes: int32 [4, 64, 4], P(None, 'req'), may hold values from 0 to 15, all different within a row; in each aligned block of 8 rows (0 to 7, 8 to 15, ..., all dimensions but the last counted through in order) at most 4 rows name the same one
- head_sink_logits: float32 [32], P('tp'), may hold values from 1 to 6
- out_weight: bfloat16 [2048, 2880], P('tp'), may hold values from -0.5 to 0.5
- mlp_gain: float32 [2880], replicated, may hold values from 0.5 to 1.5
- router_weight: bfloat16 [2880, 16], replicated, may hold values from -0.21875 to 0.21875
- expert_gate: bfloat16 [16, 2880, 2880], P('req', None, 'tp'), may hold values from -0.4375 to 0.4375
- expert_up: bfloat16 [16, 2880, 2880], P('req', None, 'tp'), may hold values from -0.4375 to 0.4375
- expert_down: bfloat16 [16, 2880, 2880], P('req', 'tp'), may hold values from -0.109375 to 0.109375
- next_gain: float32 [2880], replicated, may hold values from 0.5 to 1.5
- next_q_weight: bfloat16 [2880, 2048], P(None, 'tp'), may hold values from -0.109375 to 0.109375
- following_key_value_weight: bfloat16 [2880, 2, 512], P(None, None, 'tp'), may hold values from -0.109375 to 0.109375
Outputs:
- layer_out: bfloat16 [4, 64, 2880], P(None, 'req')
- next_query: bfloat16 [4, 64, 2048], P(None, 'req', 'tp')
- next_keyval: bfloat16 [4, 64, 2, 512], P(None, 'req', None, 'tp')
The draws below stay inside these ranges and needn't reach their ends.
Inputs may be any that keep to these rules, and one draw needn't show every extreme that they name: `lengths`: some group's prompt holds exactly 2048 positions. `routes`: a row names 4 different experts; in the rows of one device at one step no expert is named more than 4 times, a bound that some block reaches.
All inputs are finite; a program needn't handle non-finite values.
Results may differ from the reference program's by a relative error of at most 0.029.
Values may be sent and summed in bfloat16 or wider, within the bound.
A program may use at most 128 MiB of HBM per device.

```python
import math
import jax
import jax.numpy as jnp
import numpy as np
from jax import lax

MODEL_WIDTH = 2880
QUERY_HEADS = 32
KEY_VALUE_HEADS = 8
HEAD_WIDTH = 64
FF = 2880
EXPERTS = 16
TOPK = 4
GROUP_BEAMS = 8
BEAM_DEV = 8
CONTEXT_LENGTH = 2048
GENERATED_COUNT = 64
DECODE_STEPS = 4
MOST = 4
BEAM_GROUPS = 8
TOTAL_BEAMS = 64
PROMPT_SPAN = 256
SHORT = 128
SLABS = 16
ESPLIT = 1
FFS = 2880
CAPX = 32


def draw_rotated_prompt_keys(key, part):
    rotary_base = jax.random.normal(key, (TOTAL_BEAMS, PROMPT_SPAN, KEY_VALUE_HEADS * HEAD_WIDTH), jnp.float32)
    rotary_base = jnp.clip(rotary_base, -6.0, 6.0)
    return rotary_base.astype(jnp.bfloat16)


def draw_lengths(key, part):
    drawn = jax.random.randint(key, (BEAM_GROUPS,), SHORT, CONTEXT_LENGTH + 1)
    order = jax.random.permutation(jax.random.fold_in(key, 7), BEAM_GROUPS)
    drawn = drawn.at[order[0]].set(CONTEXT_LENGTH)
    return drawn.astype(jnp.int32)


def with_ends(entries, key, least, top_value):
    longest = entries.shape.index(max(entries.shape))
    spots = []
    for shift in (0, 1):
        where = [jax.random.randint(jax.random.fold_in(key, axis), (), 0, length) for axis, length in enumerate(entries.shape)]
        where[longest] = (where[longest] + shift) % entries.shape[longest]
        spots.append(tuple(where))
    return entries.at[spots[0]].set(least).at[spots[1]].set(top_value)


def shard_levels(key, shape, split, low, high):
    def one(position, blocks):
        draws = jax.random.uniform(jax.random.fold_in(jax.random.fold_in(key, 6), position), (blocks,), jnp.float32, low / len(split), high / len(split))
        return jnp.repeat(jnp.exp(draws), shape[position] // blocks).reshape((-1,) + (1,) * (len(shape) - position - 1))

    level = one(*split[0])
    for cut in split[1:]:
        level = level * one(*cut)
    return level


def deal_out(key, own, number, rows, amount, top, reach, lean):
    order = jax.random.permutation(key, amount)
    packed, common = load_shares(amount, rows * top, reach, lean, True), load_shares(amount, rows * top, reach, lean, False)
    places = jnp.arange(amount)

    def named(sizes, turn):
        used = int((sizes > 0).sum())
        fixed = max(1, used // 4)
        shifted = fixed + (places - fixed + turn * (used - fixed)) % max(1, amount - fixed)
        return jnp.zeros((amount,), jnp.int32).at[order[jnp.where(places < fixed, places, shifted)]].set(jnp.asarray(sizes, jnp.int32))

    sizes = jnp.where(number % 4 == 0, named(packed, number // 4), named(common, number - number // 4 - 1))
    mixed = jax.random.permutation(jax.random.fold_in(own, 3), amount)
    source_of, receiver = mixed[0:amount // 2 * 2:2], mixed[1:amount // 2 * 2:2]
    slack = jnp.minimum(sizes[source_of] - 1, reach - sizes[receiver]) // 2
    slack = jnp.where((source_of == order[0]) | (receiver == order[0]) | (sizes[receiver] == 0), 0, jnp.maximum(slack, 0))
    shifted = jax.random.randint(jax.random.fold_in(own, 4), (amount // 2,), 0, 1 << 20) % (slack + 1)
    sizes = sizes.at[source_of].add(-shifted).at[receiver].add(shifted)
    members = jnp.searchsorted(jnp.cumsum(sizes), jnp.arange(rows * top), side="right").astype(jnp.int32)
    grid = members.reshape(top, rows).T
    grid = grid[jax.random.permutation(jax.random.fold_in(own, 1), rows)]
    turn = jax.random.randint(jax.random.fold_in(own, 2), (rows, 1), 0, top)
    return jnp.take_along_axis(grid, (jnp.arange(top)[None, :] + turn) % top, axis=1)


def load_shares(amount, total, bound, lean, full):
    weights = [(1 << 20) // math.isqrt(rank ** lean) + 1 for rank in range(1, amount + 1)]
    largest = bound if full else min(bound, max(-(-total // amount), total * weights[0] // sum(weights)))
    least = 1 if total - largest >= amount - 1 else 0
    counts, rest = [largest] + [least] * (amount - 1), total - largest - least * (amount - 1)
    while rest > 0:
        free = [i for i in range(1, amount) if counts[i] < largest] or [i for i in range(1, amount) if counts[i] < bound]
        mass, budget = sum([weights[i] for i in free]), rest
        for i in free:
            extra = min(bound - counts[i], max(1, budget * weights[i] // mass), rest)
            counts[i] = counts[i] + extra
            rest = rest - extra
    return np.array(counts)


def bell_draw(own_key, dims, scale, most, shards=(), held_as=jnp.bfloat16):
    entries = scale * jax.random.normal(own_key, dims, jnp.float32)
    if shards:
        entries = entries * shard_levels(own_key, dims, shards, -0.22, 0.18)
    return jnp.clip(entries, -most, most).astype(held_as)


def setup_inputs(seed: int = 0) -> dict:
    seeds = jax.random.split(jax.random.key(seed), 22)
    layer_in = bell_draw(seeds[0], (DECODE_STEPS, TOTAL_BEAMS, MODEL_WIDTH), 0.5, 3.0, ((1, 8),))
    query_in = bell_draw(seeds[1], (DECODE_STEPS, TOTAL_BEAMS, QUERY_HEADS * HEAD_WIDTH), 1.0, 6.0, ((1, 8), (2, 4)))
    unrotated_key = bell_draw(seeds[2], (DECODE_STEPS, TOTAL_BEAMS, KEY_VALUE_HEADS * HEAD_WIDTH), 1.0, 6.0, ((1, 8), (2, 4)))
    incoming_value = bell_draw(seeds[3], (DECODE_STEPS, TOTAL_BEAMS, KEY_VALUE_HEADS * HEAD_WIDTH), 2.0, 12.0, ((1, 8), (2, 4)))
    rotated_prompt_keys = draw_rotated_prompt_keys(jax.random.fold_in(seeds[21], 71), 0)
    prompt_value_rows = bell_draw(seeds[5], (TOTAL_BEAMS, PROMPT_SPAN, KEY_VALUE_HEADS * HEAD_WIDTH), 1.0, 6.0, ((0, 8), (2, 4)))
    generated_key_rows = bell_draw(seeds[6], (TOTAL_BEAMS, GENERATED_COUNT, KEY_VALUE_HEADS * HEAD_WIDTH), 1.5, 9.0, ((0, 8), (2, 4)))
    generated_value_rows = bell_draw(seeds[7], (TOTAL_BEAMS, GENERATED_COUNT, KEY_VALUE_HEADS * HEAD_WIDTH), 2.0, 12.0, ((0, 8), (2, 4)))
    lengths = draw_lengths(jax.random.fold_in(seeds[21], 71), 0)
    parents = with_ends(jax.random.randint(seeds[9], (DECODE_STEPS, BEAM_GROUPS, GROUP_BEAMS), 0, GROUP_BEAMS), jax.random.fold_in(seeds[9], 1), 0, GROUP_BEAMS - 1).astype(jnp.int32)
    routes_keys = jax.random.split(jax.random.fold_in(seeds[10], 1), DECODE_STEPS * TOTAL_BEAMS // BEAM_DEV)
    routes_turns = jax.random.permutation(jax.random.fold_in(seeds[10], 3), DECODE_STEPS * TOTAL_BEAMS // BEAM_DEV)
    routes = jax.vmap(lambda own, number: deal_out(jax.random.fold_in(seeds[10], 2), own, number, BEAM_DEV, EXPERTS, TOPK, MOST, 2))(routes_keys, routes_turns).reshape((DECODE_STEPS, TOTAL_BEAMS, TOPK))
    head_sink_logits = jnp.clip(1.0 + 5.0 * jax.random.uniform(seeds[11], (QUERY_HEADS,), jnp.float32) ** shard_levels(seeds[11], (QUERY_HEADS,), ((0, 4),), -0.2, 0.2), 1.0, 6.0)
    out_weight = bell_draw(seeds[12], (QUERY_HEADS * HEAD_WIDTH, MODEL_WIDTH), (QUERY_HEADS * HEAD_WIDTH // 16) ** -0.5, 0.5, ((0, 4),))
    mlp_gain = jnp.clip(1.0 + 0.1 * jax.random.normal(seeds[13], (MODEL_WIDTH,), jnp.float32), 0.5, 1.5)
    router_weight = bell_draw(seeds[14], (MODEL_WIDTH, EXPERTS), (MODEL_WIDTH // 4) ** -0.5, 0.21875)
    expert_gate = bell_draw(seeds[15], (SLABS, MODEL_WIDTH, FFS), (MODEL_WIDTH // 16) ** -0.5, 0.4375, ((0, 8), (2, 4)))
    expert_up = bell_draw(seeds[16], (SLABS, MODEL_WIDTH, FFS), (MODEL_WIDTH // 16) ** -0.5, 0.4375, ((0, 8), (2, 4)))
    expert_down = bell_draw(seeds[17], (SLABS, FFS, MODEL_WIDTH), FF ** -0.5, 0.109375, ((0, 8), (1, 4)))
    next_gain = jnp.clip(1.0 + 0.1 * jax.random.normal(seeds[18], (MODEL_WIDTH,), jnp.float32), 0.5, 1.5)
    next_q_weight = bell_draw(seeds[19], (MODEL_WIDTH, QUERY_HEADS * HEAD_WIDTH), MODEL_WIDTH ** -0.5, 0.109375, ((1, 4),))
    following_key_value_weight = bell_draw(seeds[20], (MODEL_WIDTH, 2, KEY_VALUE_HEADS * HEAD_WIDTH), MODEL_WIDTH ** -0.5, 0.109375, ((2, 4),))
    return dict(layer_in=layer_in, query_in=query_in, unrotated_key=unrotated_key, incoming_value=incoming_value, rotated_prompt_keys=rotated_prompt_keys, prompt_value_rows=prompt_value_rows, generated_key_rows=generated_key_rows, generated_value_rows=generated_value_rows, lengths=lengths, parents=parents, routes=routes, head_sink_logits=head_sink_logits, out_weight=out_weight, mlp_gain=mlp_gain, router_weight=router_weight, expert_gate=expert_gate, expert_up=expert_up, expert_down=expert_down, next_gain=next_gain, next_q_weight=next_q_weight, following_key_value_weight=following_key_value_weight)


theta_base = 150000.0
norm_eps = 1e-05
neg_big = -1e+30
score_scale = 0.125
clamp_top = 7.0
glu_alpha = 1.702

def apply_rotary(vectors, token_positions):
    width = vectors.shape[-1]
    middle = width // 2
    powers = jnp.arange(middle, dtype=jnp.float32) * (2.0 / width)
    angles = token_positions.astype(jnp.float32)[:, None, None] * jnp.power(theta_base, -powers)
    cosine = jnp.cos(angles)
    sine_val = jnp.sin(angles)
    lower = vectors[..., :middle]
    upper = vectors[..., middle:]
    return jnp.concatenate([lower * cosine - upper * sine_val, lower * sine_val + upper * cosine], axis=-1)

def rms_scale(vectors, gain):
    mean_square = lax.optimization_barrier(jnp.mean(vectors * vectors, axis=-1, keepdims=True))
    return vectors * lax.rsqrt(mean_square + norm_eps) * gain

def rounded_f32(weights):
    return lax.optimization_barrier(weights.astype(jnp.bfloat16)).astype(jnp.float32)

def reference(layer_in, query_in, unrotated_key, incoming_value, rotated_prompt_keys, prompt_value_rows, generated_key_rows, generated_value_rows, lengths, parents, routes, head_sink_logits, out_weight, mlp_gain, router_weight, expert_gate, expert_up, expert_down, next_gain, next_q_weight, following_key_value_weight):
    query_per_key_head = QUERY_HEADS // KEY_VALUE_HEADS
    group_ids = jnp.arange(BEAM_GROUPS, dtype=jnp.int32)
    prompt_key_block = rotated_prompt_keys.reshape(GROUP_BEAMS, BEAM_GROUPS, PROMPT_SPAN, KEY_VALUE_HEADS, HEAD_WIDTH).transpose(1, 0, 2, 3, 4).reshape(BEAM_GROUPS, CONTEXT_LENGTH, KEY_VALUE_HEADS, HEAD_WIDTH)
    prompt_value_block = prompt_value_rows.reshape(GROUP_BEAMS, BEAM_GROUPS, PROMPT_SPAN, KEY_VALUE_HEADS, HEAD_WIDTH).transpose(1, 0, 2, 3, 4).reshape(BEAM_GROUPS, CONTEXT_LENGTH, KEY_VALUE_HEADS, HEAD_WIDTH)
    prompt_pos = jnp.arange(CONTEXT_LENGTH, dtype=jnp.int32)
    present_key_rows = generated_key_rows.reshape(GROUP_BEAMS, BEAM_GROUPS, GENERATED_COUNT, KEY_VALUE_HEADS, HEAD_WIDTH)
    present_value_rows = generated_value_rows.reshape(GROUP_BEAMS, BEAM_GROUPS, GENERATED_COUNT, KEY_VALUE_HEADS, HEAD_WIDTH)
    latest_key_rows = jnp.zeros((GROUP_BEAMS, BEAM_GROUPS, 0, KEY_VALUE_HEADS, HEAD_WIDTH), jnp.bfloat16)
    latest_value_rows = jnp.zeros((GROUP_BEAMS, BEAM_GROUPS, 0, KEY_VALUE_HEADS, HEAD_WIDTH), jnp.bfloat16)
    sink_score_table = head_sink_logits.reshape(KEY_VALUE_HEADS, query_per_key_head)

    def attend_group(inputs):
        queries, keys_prompt, values_prompt, length_now, keys_gen, values_gen, keys_recent, values_recent = inputs
        query_f = queries.astype(jnp.float32)
        usable = (prompt_pos < length_now)[None, None, None, :]
        scores_prompt = jnp.einsum('bhrd,shd->bhrs', query_f, keys_prompt.astype(jnp.float32)) * score_scale
        scores_prompt = jnp.where(usable, scores_prompt, neg_big)
        scores_gen = jnp.einsum('bhrd,bshd->bhrs', query_f, keys_gen.astype(jnp.float32)) * score_scale
        scores_recent = jnp.einsum('bhrd,bshd->bhrs', query_f, keys_recent.astype(jnp.float32)) * score_scale
        highest = jnp.maximum(jnp.maximum(lax.optimization_barrier(jnp.max(scores_prompt, -1)), lax.optimization_barrier(jnp.max(scores_gen, -1))), lax.optimization_barrier(jnp.max(scores_recent, -1)))
        highest = jnp.maximum(highest, sink_score_table[None])
        weights_prompt = jnp.where(usable, jnp.exp(scores_prompt - highest[..., None]), 0.0)
        weights_gen = jnp.exp(scores_gen - highest[..., None])
        weights_recent = jnp.exp(scores_recent - highest[..., None])
        denominator = lax.optimization_barrier(jnp.sum(weights_prompt, -1)) + lax.optimization_barrier(jnp.sum(weights_gen, -1)) + lax.optimization_barrier(jnp.sum(weights_recent, -1)) + jnp.exp(sink_score_table[None] - highest)
        summed = jnp.einsum('bhrs,shd->bhrd', rounded_f32(weights_prompt), values_prompt.astype(jnp.float32))
        summed = summed + jnp.einsum('bhrs,bshd->bhrd', rounded_f32(weights_gen), values_gen.astype(jnp.float32))
        summed = summed + jnp.einsum('bhrs,bshd->bhrd', rounded_f32(weights_recent), values_recent.astype(jnp.float32))
        return (summed / denominator[..., None]).astype(jnp.bfloat16)
    outputs_layer = []
    outputs_query = []
    key_value_outputs = []
    for current_step in range(DECODE_STEPS):
        pick = parents[current_step].T
        present_key_rows = present_key_rows[pick, group_ids[None, :]]
        present_value_rows = present_value_rows[pick, group_ids[None, :]]
        latest_key_rows = latest_key_rows[pick, group_ids[None, :]]
        latest_value_rows = latest_value_rows[pick, group_ids[None, :]]
        token_positions = jnp.tile(lengths + GENERATED_COUNT + current_step, GROUP_BEAMS)
        query_vector = apply_rotary(query_in[current_step].astype(jnp.float32).reshape(TOTAL_BEAMS, QUERY_HEADS, HEAD_WIDTH), token_positions).astype(jnp.bfloat16)
        newest_key = apply_rotary(unrotated_key[current_step].astype(jnp.float32).reshape(TOTAL_BEAMS, KEY_VALUE_HEADS, HEAD_WIDTH), token_positions).astype(jnp.bfloat16)
        latest_key_rows = jnp.concatenate([latest_key_rows, newest_key.reshape(GROUP_BEAMS, BEAM_GROUPS, 1, KEY_VALUE_HEADS, HEAD_WIDTH)], axis=2)
        latest_value_rows = jnp.concatenate([latest_value_rows, incoming_value[current_step].reshape(GROUP_BEAMS, BEAM_GROUPS, 1, KEY_VALUE_HEADS, HEAD_WIDTH)], axis=2)
        grouped_queries = query_vector.reshape(GROUP_BEAMS, BEAM_GROUPS, KEY_VALUE_HEADS, query_per_key_head, HEAD_WIDTH).transpose(1, 0, 2, 3, 4)
        attended = lax.map(attend_group, (grouped_queries, prompt_key_block, prompt_value_block, lengths, present_key_rows.transpose(1, 0, 2, 3, 4), present_value_rows.transpose(1, 0, 2, 3, 4), latest_key_rows.transpose(1, 0, 2, 3, 4), latest_value_rows.transpose(1, 0, 2, 3, 4)))
        attended = attended.transpose(1, 0, 2, 3, 4).reshape(TOTAL_BEAMS, QUERY_HEADS * HEAD_WIDTH)
        residual_mid = layer_in[current_step].astype(jnp.float32) + jnp.dot(attended, out_weight, preferred_element_type=jnp.float32)
        normed = rms_scale(residual_mid, mlp_gain).astype(jnp.bfloat16)
        logits = jnp.dot(normed, router_weight, preferred_element_type=jnp.float32)
        chosen = routes[current_step]
        gate_weights = jax.nn.softmax(jnp.take_along_axis(logits, chosen, axis=1), axis=-1)

        def slab_step(slab, running):
            expert_id = slab // ESPLIT
            matched = chosen == expert_id
            weight_rows = lax.optimization_barrier(jnp.sum(jnp.where(matched, gate_weights, 0.0), axis=1))
            used_rows = jnp.any(matched, axis=1)
            picked_rows = jnp.nonzero(used_rows, size=CAPX, fill_value=0)[0].astype(jnp.int32)
            used_count = jnp.sum(used_rows.astype(jnp.int32))
            rows_in = normed[picked_rows]
            gate_val = jnp.minimum(jnp.dot(rows_in, expert_gate[slab], preferred_element_type=jnp.float32), clamp_top)
            up_val = jnp.clip(jnp.dot(rows_in, expert_up[slab], preferred_element_type=jnp.float32), -clamp_top, clamp_top)
            hidden = ((up_val + 1.0) * gate_val * jax.nn.sigmoid(glu_alpha * gate_val)).astype(jnp.bfloat16)
            rows_out = jnp.dot(hidden, expert_down[slab], preferred_element_type=jnp.float32)
            scale_rows = jnp.where(jnp.arange(CAPX, dtype=jnp.int32) < used_count, weight_rows[picked_rows], 0.0)
            return running.at[picked_rows].add(rows_out * scale_rows[:, None])
        moe_total = lax.fori_loop(0, SLABS, slab_step, jnp.zeros((TOTAL_BEAMS, MODEL_WIDTH), jnp.float32))
        residual_out = residual_mid + moe_total
        outputs_layer.append(residual_out.astype(jnp.bfloat16))
        last_normed_state = rms_scale(residual_out, next_gain).astype(jnp.bfloat16)
        outputs_query.append(jnp.dot(last_normed_state, next_q_weight, preferred_element_type=jnp.float32).astype(jnp.bfloat16))
        flat_key_value = jnp.dot(last_normed_state, following_key_value_weight.reshape(MODEL_WIDTH, 2 * KEY_VALUE_HEADS * HEAD_WIDTH), preferred_element_type=jnp.float32)
        key_value_outputs.append(flat_key_value.astype(jnp.bfloat16).reshape(TOTAL_BEAMS, 2, KEY_VALUE_HEADS * HEAD_WIDTH))
    return (jnp.stack(outputs_layer), jnp.stack(outputs_query), jnp.stack(key_value_outputs))
```

```python
import jax
import jax.numpy as jnp
from jax import lax
from jax.sharding import PartitionSpec as P

HEAD = 64
EXPERTS = 16
THETA = 150000.0
EPS = 1e-05
NEG = -1e30
BF = jnp.bfloat16
F32 = jnp.float32


def rope(vectors, positions):
    half = HEAD // 2
    powers = jnp.arange(half, dtype=F32) * (2.0 / HEAD)
    angles = positions.astype(F32)[..., None, None] * jnp.power(THETA, -powers)
    cos, sin = jnp.cos(angles), jnp.sin(angles)
    lower, upper = vectors[..., :half], vectors[..., half:]
    return jnp.concatenate([lower * cos - upper * sin, lower * sin + upper * cos], axis=-1)


def rms(rows, gain):
    return rows * lax.rsqrt(jnp.mean(rows * rows, axis=-1, keepdims=True) + EPS) * gain


def lineage_tables(parents):
    steps, groups, beams = parents.shape
    ident = jnp.broadcast_to(jnp.arange(beams, dtype=jnp.int32), (groups, beams))
    first = []
    tokens = [[None] * steps for _ in range(steps)]
    for t in range(steps):
        walker = ident
        for s in range(t, -1, -1):
            tokens[s][t] = walker
            hot = walker[..., None] == jnp.arange(beams, dtype=jnp.int32)
            walker = jnp.sum(jnp.where(hot, parents[s][:, None, :], 0), axis=-1)
        first.append(walker)
        for s in range(t + 1, steps):
            tokens[s][t] = jnp.full_like(ident, -1)
    return jnp.stack(first), jnp.stack([jnp.stack(row) for row in tokens])


def local(
    layer_in, query_in, key_in, value_in, prompt_keys, prompt_values, gen_keys, gen_values,
    lengths, parents, routes, sinks, out_weight, mlp_gain, router_weight,
    expert_gate, expert_up, expert_down, next_gain, next_q_weight, next_kv_weight,
):
    req_count = lax.axis_size("req")
    me = lax.axis_index("req")
    T, B, q_width = query_in.shape
    kv_width = key_in.shape[2]
    K = kv_width // HEAD
    R = q_width // kv_width
    J = parents.shape[2]
    span = req_count // J
    beam = me // span
    start = me % span * B
    groups = [[c + span * j for j in range(J)] for c in range(span)]
    if span == 1:
        groups = None
    lens = lax.dynamic_slice_in_dim(lengths, start, B)
    pars = lax.dynamic_slice_in_dim(parents, start, B, axis=1)
    S = prompt_keys.shape[1]
    G = gen_keys.shape[1]
    pos = lens[None, :] + G + jnp.arange(T, dtype=jnp.int32)[:, None]
    q = rope(query_in.astype(F32).reshape(T, B, K * R, HEAD), pos).astype(BF).reshape(T, B, q_width)
    k = rope(key_in.astype(F32).reshape(T, B, K, HEAD), pos).astype(BF).reshape(T, B, kv_width)
    q_all = lax.all_gather(q, "req", axis_index_groups=groups)
    first, tokens = lineage_tables(pars)
    prompt_ok = (beam * S + jnp.arange(S, dtype=jnp.int32))[None, :] < lens[:, None]
    mask = jnp.concatenate(
        [
            jnp.broadcast_to(prompt_ok[:, None, None, :], (B, J, T, S)),
            jnp.broadcast_to((first == beam).transpose(1, 2, 0)[..., None], (B, J, T, G)),
            (tokens == beam).transpose(2, 3, 1, 0),
        ],
        axis=-1,
    )
    keys = jnp.concatenate([prompt_keys, gen_keys, k.transpose(1, 0, 2)], axis=1)
    values = jnp.concatenate([prompt_values, gen_values, value_in.transpose(1, 0, 2)], axis=1)
    keys = keys.reshape(B, S + G + T, K, HEAD)
    values = values.reshape(B, S + G + T, K, HEAD)
    qs = q_all.reshape(J, T, B, K, R, HEAD)
    scores = jnp.einsum("jtbkrd,bskd->bkjtrs", qs, keys, preferred_element_type=F32) * 0.125
    usable = mask[:, None, :, :, None, :]
    scores = jnp.where(usable, scores, NEG)
    high = jnp.max(scores, axis=-1)
    weights = jnp.where(usable, jnp.exp(scores - high[..., None]), 0.0)
    total = jnp.sum(weights, axis=-1)
    part = jnp.einsum("bkjtrs,bskd->jtbkrd", weights.astype(BF), values, preferred_element_type=F32)
    high = high.transpose(2, 3, 0, 1, 4)
    total = total.transpose(2, 3, 0, 1, 4)
    part = (part / jnp.maximum(total, 1e-30)[..., None]).astype(BF)
    stats = jnp.stack([high, total], axis=1)
    part = lax.all_to_all(part, "req", 0, 0, axis_index_groups=groups)
    stats = lax.all_to_all(stats, "req", 0, 0, axis_index_groups=groups)
    high, total = stats[:, 0], stats[:, 1]
    sink = sinks.reshape(K, R)
    peak = jnp.maximum(jnp.max(high, axis=0), sink)
    share = total * jnp.exp(high - peak)
    bottom = jnp.sum(share, axis=0) + jnp.exp(sink - peak)
    attended = jnp.sum(part.astype(F32) * (share / bottom)[..., None], axis=0)
    attended = attended.astype(BF).reshape(T * B, q_width)
    projected = jnp.dot(attended, out_weight, preferred_element_type=F32)
    x1 = layer_in.reshape(T * B, -1).astype(F32) + lax.psum(projected.astype(BF), "tp").astype(F32)
    h2 = rms(x1, mlp_gain).astype(BF)
    logits = jnp.dot(h2, router_weight, preferred_element_type=F32)
    hot = jnp.sum(
        (routes.reshape(T * B, -1, 1) == jnp.arange(EXPERTS, dtype=jnp.int32)).astype(F32), axis=1
    )
    masked = jnp.where(hot > 0, logits, NEG)
    raw = jnp.where(hot > 0, jnp.exp(masked - jnp.max(masked, axis=-1, keepdims=True)), 0.0)
    gates = raw / jnp.sum(raw, axis=-1, keepdims=True)
    h2_all = lax.all_gather(h2, "req", tiled=True)
    gates_all = lax.all_gather(gates, "req", tiled=True)
    slabs = expert_gate.shape[0]
    split = slabs * req_count // EXPERTS
    moe = 0.0
    for s in range(slabs):
        expert = (me * slabs + s) // split
        weight = lax.dynamic_slice_in_dim(gates_all, expert, 1, axis=1)
        gate = jnp.minimum(jnp.dot(h2_all, expert_gate[s], preferred_element_type=F32), 7.0)
        up = jnp.clip(jnp.dot(h2_all, expert_up[s], preferred_element_type=F32), -7.0, 7.0)
        hidden = ((up + 1.0) * gate * jax.nn.sigmoid(1.702 * gate) * weight).astype(BF)
        moe = moe + jnp.dot(hidden, expert_down[s], preferred_element_type=F32)
    moe = lax.psum_scatter(moe.astype(BF), "req", scatter_dimension=0, tiled=True)
    moe = lax.psum(moe, "tp").astype(F32)
    x2 = x1 + moe
    h3 = rms(x2, next_gain).astype(BF)
    next_query = jnp.dot(h3, next_q_weight, preferred_element_type=F32).astype(BF)
    next_kv = jnp.einsum("nd,dcf->ncf", h3, next_kv_weight, preferred_element_type=F32).astype(BF)
    return (
        x2.astype(BF).reshape(T, B, -1),
        next_query.reshape(T, B, q_width),
        next_kv.reshape(T, B, 2, kv_width),
    )


def solution(mesh):
    placed = (
        P(None, "req", None), P(None, "req", "tp"), P(None, "req", "tp"), P(None, "req", "tp"),
        P("req", None, "tp"), P("req", None, "tp"), P("req", None, "tp"), P("req", None, "tp"),
        P(), P(), P(None, "req", None), P("tp"), P("tp", None), P(), P(),
        P("req", None, "tp"), P("req", None, "tp"), P("req", "tp", None),
        P(), P(None, "tp"), P(None, None, "tp"),
    )
    return jax.shard_map(
        local, mesh=mesh, in_specs=placed,
        out_specs=(P(None, "req", None), P(None, "req", "tp"), P(None, "req", None, "tp")),
        check_vma=False,
    )
```

```python
import functools

import jax
import jax.numpy as jnp
from jax import lax
from jax.experimental import pallas as pl
from jax.experimental.pallas import tpu as pltpu
from jax.sharding import PartitionSpec as P

HEAD = 64
EXPERTS = 16
THETA = 150000.0
EPS = 1e-05
NEG = -1e30
BF = jnp.bfloat16
F32 = jnp.float32


def rope(vectors, positions):
    half = HEAD // 2
    powers = jnp.arange(half, dtype=F32) * (2.0 / HEAD)
    angles = positions.astype(F32)[..., None, None] * jnp.power(THETA, -powers)
    cos, sin = jnp.cos(angles), jnp.sin(angles)
    lower, upper = vectors[..., :half], vectors[..., half:]
    return jnp.concatenate([lower * cos - upper * sin, lower * sin + upper * cos], axis=-1)


def rms(rows, gain):
    return rows * lax.rsqrt(jnp.mean(rows * rows, axis=-1, keepdims=True) + EPS) * gain


def lineage_tables(parents):
    steps, groups, beams = parents.shape
    ident = jnp.broadcast_to(jnp.arange(beams, dtype=jnp.int32), (groups, beams))
    first = []
    tokens = [[None] * steps for _ in range(steps)]
    for t in range(steps):
        walker = ident
        for s in range(t, -1, -1):
            tokens[s][t] = walker
            hot = walker[..., None] == jnp.arange(beams, dtype=jnp.int32)
            walker = jnp.sum(jnp.where(hot, parents[s][:, None, :], 0), axis=-1)
        first.append(walker)
        for s in range(t + 1, steps):
            tokens[s][t] = jnp.full_like(ident, -1)
    return jnp.stack(first), jnp.stack([jnp.stack(row) for row in tokens])


CH = 768
EX = 128
HOT0 = 16


def tail_kernel(
    nreq, slabs, width,
    att_ref, lin_ref, hot_ref, wo_hbm, mg_ref, wr_ref, wg_hbm, wu_hbm, wd_hbm, ng_ref, wq_hbm, wk_hbm,
    lo_ref, nq_ref, nk_ref,
    wo, wg, wu, wd, wq, wk,
    psrc, prcv, xs, gs, yall, part, rb1, sb2, rb2, sb3, rb3, x2a,
    wsem, psnd, prsem, gsnd, grcv, ysnd, yrcv, csnd, crcv,
    asnd, arcv, bsnd, brcv, dsnd, drcv, fsnd, frcv,
):
    me = lax.axis_index("req")
    tp = lax.axis_index("tp")
    core, yy = tp % 2, tp // 2
    rows = att_ref.shape[0]

    def peer(d):
        return ((yy + d // 2) % 2) * 2 + (core + d % 2) % 2

    def rcopy(src, dst, ssem, rsem, req, t):
        return pltpu.make_async_remote_copy(
            src_ref=src, dst_ref=dst, send_sem=ssem, recv_sem=rsem,
            device_id=(req, t), device_id_type=pl.DeviceIdType.MESH,
        )

    loads = [pltpu.make_async_copy(wo_hbm, wo, wsem.at[0])]
    for s in range(slabs):
        loads.append(pltpu.make_async_copy(wg_hbm.at[s], wg.at[s], wsem.at[1 + 3 * s]))
        loads.append(pltpu.make_async_copy(wu_hbm.at[s], wu.at[s], wsem.at[2 + 3 * s]))
    for s in range(slabs):
        loads.append(pltpu.make_async_copy(wd_hbm.at[s], wd.at[s], wsem.at[3 + 3 * s]))
    loads.append(pltpu.make_async_copy(wq_hbm, wq, wsem.at[1 + 3 * slabs]))
    loads.append(pltpu.make_async_copy(wk_hbm, wk, wsem.at[2 + 3 * slabs]))
    for copy in loads:
        copy.start()

    barrier = pltpu.get_barrier_semaphore()
    for i in range(1, nreq):
        pl.semaphore_signal(
            barrier, inc=1, device_id=((me + i) % nreq, tp), device_id_type=pl.DeviceIdType.MESH
        )
    for d in range(1, 4):
        pl.semaphore_signal(
            barrier, inc=1, device_id=(me, peer(d)), device_id_type=pl.DeviceIdType.MESH
        )

    spans = []
    at = 0
    while at < width:
        spans.append((at, min(CH, width - at)))
        at += CH

    def blk(r):
        return pl.ds(pl.multiple_of(r * rows, rows), rows)

    loads[0].wait()
    att = att_ref[...]
    for c, (a, w) in enumerate(spans):
        if w < CH:
            psrc[c] = jnp.zeros((rows, CH), BF)
            xs[c] = jnp.zeros((rows, CH), F32)
            gs[c] = jnp.zeros((8, CH), F32)
        psrc[c, :, :w] = jnp.dot(att, wo[:, a:a + w], preferred_element_type=F32).astype(BF)
        xs[c, :, :w] = lin_ref[:, a:a + w].astype(F32)
        gs[c, :, :w] = jnp.broadcast_to(mg_ref[:, a:a + w], (8, w))
    pl.semaphore_wait(barrier, nreq - 1 + 3)
    sends = []
    for d in (2, 3, 1):
        cp = rcopy(psrc.at[peer(d)], prcv.at[d - 1], psnd.at[d - 1], prsem.at[d - 1], me, peer(d))
        cp.start()
        sends.append(cp)
    x1 = xs[tp] + psrc[tp].astype(F32)
    for cp in sends:
        cp.wait()
    for d in range(3):
        x1 = x1 + prcv[d].astype(F32)
    xs[tp] = x1
    lane = lax.broadcasted_iota(jnp.int32, (rows, EX), 1)
    ssq = jnp.sum(x1 * x1, axis=1, keepdims=True)
    high = ssq.astype(BF).astype(F32)
    low = ssq - high
    extra = jnp.where(lane == 0, high, jnp.where(lane == 1, low, hot_ref[...]))
    yall[tp, blk(me), :CH] = (x1 * gs[tp][:1]).astype(BF)
    yall[tp, blk(me), CH:] = extra.astype(BF)

    sends = []
    for i in range(1, nreq):
        piece = yall.at[tp, blk(me)]
        cp = rcopy(piece, piece, gsnd.at[i], grcv.at[i], (me + i) % nreq, tp)
        cp.start()
        sends.append(cp)
    ty, tc, td = peer(2), peer(1), peer(3)
    for i in range(nreq):
        src = (me + nreq - i) % nreq
        piece = yall.at[tp, blk(src)]
        if i > 0:
            rcopy(piece, piece, gsnd.at[i], grcv.at[i], (me + i) % nreq, tp).wait_recv()
        cp = rcopy(piece, piece, ysnd.at[i], yrcv.at[i], me, ty)
        cp.start()
        sends.append(cp)
        cp = rcopy(piece, piece, csnd.at[0, i], crcv.at[0, i], me, tc)
        cp.start()
        sends.append(cp)
    for i in range(nreq):
        piece = yall.at[ty, blk((me + nreq - i) % nreq)]
        rcopy(piece, piece, ysnd.at[i], yrcv.at[i], me, ty).wait_recv()
        cp = rcopy(piece, piece, csnd.at[1, i], crcv.at[1, i], me, tc)
        cp.start()
        sends.append(cp)
    for i in range(nreq):
        piece = yall.at[tc, blk((me + nreq - i) % nreq)]
        rcopy(piece, piece, csnd.at[0, i], crcv.at[0, i], me, tc).wait_recv()
        piece = yall.at[td, blk((me + nreq - i) % nreq)]
        rcopy(piece, piece, csnd.at[1, i], crcv.at[1, i], me, tc).wait_recv()
    for cp in sends:
        cp.wait_send()

    total = nreq * rows
    lanes = lax.broadcasted_iota(jnp.int32, (total, EX), 1)
    ssq = jnp.zeros((total, 1), F32)
    logits = jnp.zeros((total, EX), F32)
    for c, (a, w) in enumerate(spans):
        ssq = ssq + jnp.sum(
            jnp.where(lanes < 2, yall[c, :, CH:].astype(F32), 0.0), axis=1, keepdims=True
        )
        logits = logits + jnp.dot(yall[c, :, :w], wr_ref[a:a + w, :], preferred_element_type=F32)
    scale = lax.rsqrt(ssq / width + EPS)
    logits = logits * scale
    hot = (lanes >= HOT0) & (yall[0, :, CH:].astype(F32) > 0.5)
    masked = jnp.where(hot, logits, NEG)
    raw = jnp.where(hot, jnp.exp(masked - jnp.max(masked, axis=1, keepdims=True)), 0.0)
    gates = raw / jnp.sum(raw, axis=1, keepdims=True)

    hidden = []
    for s in range(slabs):
        weight = jnp.sum(
            jnp.where(lanes == HOT0 + me * slabs + s, gates, 0.0), axis=1, keepdims=True
        )
        loads[1 + 2 * s].wait()
        loads[2 + 2 * s].wait()
        gate = 0.0
        up = 0.0
        for c, (a, w) in enumerate(spans):
            y = yall[c, :, :w]
            gate = gate + jnp.dot(y, wg[s, a:a + w, :], preferred_element_type=F32)
            up = up + jnp.dot(y, wu[s, a:a + w, :], preferred_element_type=F32)
        gate = jnp.minimum(gate * scale, 7.0)
        up = jnp.clip(up * scale, -7.0, 7.0)
        sig = 1.0 / (1.0 + jnp.exp(-1.702 * gate))
        hidden.append(((up + 1.0) * gate * sig * weight).astype(BF))
    for s in range(slabs):
        loads[1 + 2 * slabs + s].wait()
    for c, (a, w) in enumerate(spans):
        acc = 0.0
        for s in range(slabs):
            acc = acc + jnp.dot(hidden[s], wd[s, :, a:a + w], preferred_element_type=F32)
        if w < CH:
            part[c, :, w:] = jnp.zeros((total, CH - w), BF)
        part[c, :, :w] = acc.astype(BF)

    sends = []
    for k, c in ((1, td), (0, tc)):
        cp = rcopy(part.at[c], rb1.at[k], asnd.at[k], arcv.at[k], me, tc)
        cp.start()
        sends.append(cp)
    order = list(range(1, nreq)) + [0]
    sends[0].wait_recv()
    for i in order:
        b = (me + i) % nreq
        sb2[i] = (part[ty, blk(b), :].astype(F32) + rb1[1, blk(b), :].astype(F32)).astype(BF)
        cp = rcopy(sb2.at[i], rb2.at[i], bsnd.at[i], brcv.at[i], me, ty)
        cp.start()
        sends.append(cp)
    sends[1].wait_recv()
    moe = 0.0
    late = []
    for i in order:
        b = (me + i) % nreq
        mine = part[tp, blk(b), :].astype(F32) + rb1[0, blk(b), :].astype(F32)
        rcopy(sb2.at[i], rb2.at[i], bsnd.at[i], brcv.at[i], me, ty).wait_recv()
        mine = mine + rb2[i].astype(F32)
        if i == 0:
            moe = mine
        else:
            sb3[i] = mine.astype(BF)
            cp = rcopy(sb3.at[i], rb3.at[i], dsnd.at[i], drcv.at[i], b, tp)
            cp.start()
            sends.append(cp)
            late.append(cp)
    for n, cp in enumerate(late):
        cp.wait_recv()
        moe = moe + rb3[n + 1].astype(F32)
    x2a[tp] = xs[tp] + moe
    late = []
    for d in (2, 3, 1):
        cp = rcopy(x2a.at[tp], x2a.at[tp], fsnd.at[d - 1], frcv.at[d - 1], me, peer(d))
        cp.start()
        sends.append(cp)
    for d in range(1, 4):
        piece = x2a.at[peer(d)]
        rcopy(piece, piece, fsnd.at[d - 1], frcv.at[d - 1], me, peer(d)).wait_recv()
    for cp in sends:
        cp.wait_send()
    ssq = jnp.zeros((rows, 1), F32)
    for c, (a, w) in enumerate(spans):
        x2 = x2a[c, :, :w]
        lo_ref[:, a:a + w] = x2.astype(BF)
        ssq = ssq + jnp.sum(x2 * x2, axis=1, keepdims=True)
    scale = lax.rsqrt(ssq / width + EPS)
    loads[1 + 3 * slabs].wait()
    loads[2 + 3 * slabs].wait()
    nq = 0.0
    nk = 0.0
    for c, (a, w) in enumerate(spans):
        h3 = (x2a[c, :, :w] * scale * ng_ref[:, a:a + w]).astype(BF)
        nq = nq + jnp.dot(h3, wq[a:a + w, :], preferred_element_type=F32)
        nk = nk + jnp.dot(h3, wk[a:a + w, :], preferred_element_type=F32)
    nq_ref[...] = nq.astype(BF)
    nk_ref[...] = nk.astype(BF)


def tail(att, lin, hot, wo, mg, wr, wg, wu, wd, ng, wq, wk, nreq):
    rows, width = lin.shape
    slabs, _, ff = wg.shape
    total = nreq * rows
    chunks = -(-width // CH)
    vm = pl.BlockSpec(memory_space=pltpu.VMEM)
    hb = pl.BlockSpec(memory_space=pl.ANY)
    dma = pltpu.SemaphoreType.DMA
    return pl.pallas_call(
        functools.partial(tail_kernel, nreq, slabs, width),
        out_shape=(
            jax.ShapeDtypeStruct((rows, width), BF),
            jax.ShapeDtypeStruct((rows, wq.shape[1]), BF),
            jax.ShapeDtypeStruct((rows, wk.shape[1]), BF),
        ),
        in_specs=[vm, vm, vm, hb, vm, vm, hb, hb, hb, vm, hb, hb],
        out_specs=(vm, vm, vm),
        scratch_shapes=[
            pltpu.VMEM(wo.shape, BF), pltpu.VMEM(wg.shape, BF), pltpu.VMEM(wu.shape, BF),
            pltpu.VMEM(wd.shape, BF), pltpu.VMEM(wq.shape, BF), pltpu.VMEM(wk.shape, BF),
            pltpu.VMEM((chunks, rows, CH), BF),
            pltpu.VMEM((3, rows, CH), BF),
            pltpu.VMEM((chunks, rows, CH), F32),
            pltpu.VMEM((chunks, 8, CH), F32),
            pltpu.VMEM((chunks, total, CH + EX), BF),
            pltpu.VMEM((chunks, total, CH), BF),
            pltpu.VMEM((2, total, CH), BF),
            pltpu.VMEM((nreq, rows, CH), BF),
            pltpu.VMEM((nreq, rows, CH), BF),
            pltpu.VMEM((nreq, rows, CH), BF),
            pltpu.VMEM((nreq, rows, CH), BF),
            pltpu.VMEM((chunks, rows, CH), F32),
            dma((3 + 3 * slabs,)), dma((3,)), dma((3,)), dma((nreq,)), dma((nreq,)),
            dma((nreq,)), dma((nreq,)), dma((2, nreq)), dma((2, nreq)),
            dma((2,)), dma((2,)), dma((nreq,)), dma((nreq,)), dma((nreq,)), dma((nreq,)),
            dma((3,)), dma((3,)),
        ],
        compiler_params=pltpu.CompilerParams(
            collective_id=0, has_side_effects=True, vmem_limit_bytes=58 * 2**20
        ),
        cost_estimate=pl.CostEstimate(
            flops=2 * total * slabs * width * ff * 3, bytes_accessed=33 * 2**20, transcendentals=0
        ),
    )(att, lin, hot, wo, mg, wr, wg, wu, wd, ng, wq, wk)


def local(
    layer_in, query_in, key_in, value_in, prompt_keys, prompt_values, gen_keys, gen_values,
    lengths, parents, routes, sinks, out_weight, mlp_gain, router_weight,
    expert_gate, expert_up, expert_down, next_gain, next_q_weight, next_kv_weight,
):
    req_count = lax.axis_size("req")
    me = lax.axis_index("req")
    T, B, q_width = query_in.shape
    kv_width = key_in.shape[2]
    K = kv_width // HEAD
    R = q_width // kv_width
    J = parents.shape[2]
    span = req_count // J
    beam = me // span
    start = me % span * B
    groups = [[c + span * j for j in range(J)] for c in range(span)]
    if span == 1:
        groups = None
    lens = lax.dynamic_slice_in_dim(lengths, start, B)
    pars = lax.dynamic_slice_in_dim(parents, start, B, axis=1)
    S = prompt_keys.shape[1]
    G = gen_keys.shape[1]
    pos = lens[None, :] + G + jnp.arange(T, dtype=jnp.int32)[:, None]
    q = rope(query_in.astype(F32).reshape(T, B, K * R, HEAD), pos).astype(BF).reshape(T, B, q_width)
    k = rope(key_in.astype(F32).reshape(T, B, K, HEAD), pos).astype(BF).reshape(T, B, kv_width)
    q_all = lax.all_gather(q, "req", axis_index_groups=groups)
    first, tokens = lineage_tables(pars)
    prompt_ok = (beam * S + jnp.arange(S, dtype=jnp.int32))[None, :] < lens[:, None]
    mask = jnp.concatenate(
        [
            jnp.broadcast_to(prompt_ok[:, None, None, :], (B, J, T, S)),
            jnp.broadcast_to((first == beam).transpose(1, 2, 0)[..., None], (B, J, T, G)),
            (tokens == beam).transpose(2, 3, 1, 0),
        ],
        axis=-1,
    )
    keys = jnp.concatenate([prompt_keys, gen_keys, k.transpose(1, 0, 2)], axis=1)
    values = jnp.concatenate([prompt_values, gen_values, value_in.transpose(1, 0, 2)], axis=1)
    keys = keys.reshape(B, S + G + T, K, HEAD)
    values = values.reshape(B, S + G + T, K, HEAD)
    qs = q_all.reshape(J, T, B, K, R, HEAD)
    scores = jnp.einsum("jtbkrd,bskd->bkjtrs", qs, keys, preferred_element_type=F32) * 0.125
    usable = mask[:, None, :, :, None, :]
    scores = jnp.where(usable, scores, NEG)
    high = jnp.max(scores, axis=-1)
    weights = jnp.where(usable, jnp.exp(scores - high[..., None]), 0.0)
    total = jnp.sum(weights, axis=-1)
    part = jnp.einsum("bkjtrs,bskd->jtbkrd", weights.astype(BF), values, preferred_element_type=F32)
    high = high.transpose(2, 3, 0, 1, 4)
    total = total.transpose(2, 3, 0, 1, 4)
    part = (part / jnp.maximum(total, 1e-30)[..., None]).astype(BF)
    stats = jnp.stack([high, total], axis=1)
    part = lax.all_to_all(part, "req", 0, 0, axis_index_groups=groups)
    stats = lax.all_to_all(stats, "req", 0, 0, axis_index_groups=groups)
    high, total = stats[:, 0], stats[:, 1]
    sink = sinks.reshape(K, R)
    peak = jnp.maximum(jnp.max(high, axis=0), sink)
    share = total * jnp.exp(high - peak)
    bottom = jnp.sum(share, axis=0) + jnp.exp(sink - peak)
    attended = jnp.sum(part.astype(F32) * (share / bottom)[..., None], axis=0)
    attended = attended.astype(BF).reshape(T * B, q_width)
    if lax.axis_size("tp") == 4 and span == 1 and expert_gate.shape[0] * req_count == EXPERTS:
        hot = jnp.sum(
            (routes.reshape(T * B, -1, 1) == jnp.arange(EX, dtype=jnp.int32) - HOT0).astype(F32), axis=1
        )
        routing = jnp.pad(router_weight, ((0, 0), (HOT0, EX - HOT0 - EXPERTS)))
        out, nq, nk = tail(
            attended, layer_in.reshape(T * B, -1), hot, out_weight, mlp_gain[None], routing,
            expert_gate, expert_up, expert_down, next_gain[None], next_q_weight,
            next_kv_weight.reshape(-1, 2 * kv_width), req_count,
        )
        return (
            out.reshape(T, B, -1), nq.reshape(T, B, q_width), nk.reshape(T, B, 2, kv_width)
        )
    projected = jnp.dot(attended, out_weight, preferred_element_type=F32)
    x1 = layer_in.reshape(T * B, -1).astype(F32) + lax.psum(projected.astype(BF), "tp").astype(F32)
    h2 = rms(x1, mlp_gain).astype(BF)
    logits = jnp.dot(h2, router_weight, preferred_element_type=F32)
    hot = jnp.sum(
        (routes.reshape(T * B, -1, 1) == jnp.arange(EXPERTS, dtype=jnp.int32)).astype(F32), axis=1
    )
    masked = jnp.where(hot > 0, logits, NEG)
    raw = jnp.where(hot > 0, jnp.exp(masked - jnp.max(masked, axis=-1, keepdims=True)), 0.0)
    gates = raw / jnp.sum(raw, axis=-1, keepdims=True)
    h2_all = lax.all_gather(h2, "req", tiled=True)
    gates_all = lax.all_gather(gates, "req", tiled=True)
    slabs = expert_gate.shape[0]
    split = slabs * req_count // EXPERTS
    moe = 0.0
    for s in range(slabs):
        expert = (me * slabs + s) // split
        weight = lax.dynamic_slice_in_dim(gates_all, expert, 1, axis=1)
        gate = jnp.minimum(jnp.dot(h2_all, expert_gate[s], preferred_element_type=F32), 7.0)
        up = jnp.clip(jnp.dot(h2_all, expert_up[s], preferred_element_type=F32), -7.0, 7.0)
        hidden = ((up + 1.0) * gate * jax.nn.sigmoid(1.702 * gate) * weight).astype(BF)
        moe = moe + jnp.dot(hidden, expert_down[s], preferred_element_type=F32)
    moe = lax.psum_scatter(moe.astype(BF), "req", scatter_dimension=0, tiled=True)
    moe = lax.psum(moe, "tp").astype(F32)
    x2 = x1 + moe
    h3 = rms(x2, next_gain).astype(BF)
    next_query = jnp.dot(h3, next_q_weight, preferred_element_type=F32).astype(BF)
    next_kv = jnp.einsum("nd,dcf->ncf", h3, next_kv_weight, preferred_element_type=F32).astype(BF)
    return (
        x2.astype(BF).reshape(T, B, -1),
        next_query.reshape(T, B, q_width),
        next_kv.reshape(T, B, 2, kv_width),
    )


def solution(mesh):
    placed = (
        P(None, "req", None), P(None, "req", "tp"), P(None, "req", "tp"), P(None, "req", "tp"),
        P("req", None, "tp"), P("req", None, "tp"), P("req", None, "tp"), P("req", None, "tp"),
        P(), P(), P(None, "req", None), P("tp"), P("tp", None), P(), P(),
        P("req", None, "tp"), P("req", None, "tp"), P("req", "tp", None),
        P(), P(None, "tp"), P(None, None, "tp"),
    )
    return jax.shard_map(
        local, mesh=mesh, in_specs=placed,
        out_specs=(P(None, "req", None), P(None, "req", "tp"), P(None, "req", None, "tp")),
        check_vma=False,
    )
```

```python
import functools

import jax
import jax.numpy as jnp
from jax import lax
from jax.experimental import pallas as pl
from jax.experimental.pallas import tpu as pltpu
from jax.sharding import PartitionSpec as P

HEAD = 64
EXPERTS = 16
THETA = 150000.0
EPS = 1e-05
NEG = -1e30
BF = jnp.bfloat16
F32 = jnp.float32


def rope(vectors, positions):
    half = HEAD // 2
    powers = jnp.arange(half, dtype=F32) * (2.0 / HEAD)
    angles = positions.astype(F32)[..., None, None] * jnp.power(THETA, -powers)
    cos, sin = jnp.cos(angles), jnp.sin(angles)
    lower, upper = vectors[..., :half], vectors[..., half:]
    return jnp.concatenate([lower * cos - upper * sin, lower * sin + upper * cos], axis=-1)


def rms(rows, gain):
    return rows * lax.rsqrt(jnp.mean(rows * rows, axis=-1, keepdims=True) + EPS) * gain


def lineage_tables(parents):
    steps, groups, beams = parents.shape
    ident = jnp.broadcast_to(jnp.arange(beams, dtype=jnp.int32), (groups, beams))
    first = []
    tokens = [[None] * steps for _ in range(steps)]
    for t in range(steps):
        walker = ident
        for s in range(t, -1, -1):
            tokens[s][t] = walker
            hot = walker[..., None] == jnp.arange(beams, dtype=jnp.int32)
            walker = jnp.sum(jnp.where(hot, parents[s][:, None, :], 0), axis=-1)
        first.append(walker)
        for s in range(t + 1, steps):
            tokens[s][t] = jnp.full_like(ident, -1)
    return jnp.stack(first), jnp.stack([jnp.stack(row) for row in tokens])


CH = 768
EX = 128
SSQ0 = 16
NT = (((1,), (1,)), ((), ()))


def tail_kernel(
    nreq, slabs, width,
    att_ref, lin_ref, hot_ref, wo_hbm, mg_ref, wr_ref, wg_hbm, wu_hbm, wd_hbm, ng_ref, wq_hbm, wk_hbm,
    lo_ref, nq_ref, nk_ref,
    wo, wg, wu, wd, wq, wk,
    psrc, prcv, xs, gs, yall, part, rb1, sb2, rb2, sb3, rb3, x2a,
    wsem, psnd, prsem, gsnd, grcv, ysnd, yrcv, csnd, crcv,
    asnd, arcv, bsnd, brcv, dsnd, drcv, fsnd, frcv,
):
    me = lax.axis_index("req")
    tp = lax.axis_index("tp")
    core, yy = tp % 2, tp // 2
    rows = att_ref.shape[0]

    def peer(d):
        return ((yy + d // 2) % 2) * 2 + (core + d % 2) % 2

    def rcopy(src, dst, ssem, rsem, req, t):
        return pltpu.make_async_remote_copy(
            src_ref=src, dst_ref=dst, send_sem=ssem, recv_sem=rsem,
            device_id=(req, t), device_id_type=pl.DeviceIdType.MESH,
        )

    loads = [pltpu.make_async_copy(wo_hbm, wo, wsem.at[0])]
    for s in range(slabs):
        loads.append(pltpu.make_async_copy(wg_hbm.at[s], wg.at[s], wsem.at[1 + 3 * s]))
        loads.append(pltpu.make_async_copy(wu_hbm.at[s], wu.at[s], wsem.at[2 + 3 * s]))
    for s in range(slabs):
        loads.append(pltpu.make_async_copy(wd_hbm.at[s], wd.at[s], wsem.at[3 + 3 * s]))
    loads.append(pltpu.make_async_copy(wq_hbm, wq, wsem.at[1 + 3 * slabs]))
    loads.append(pltpu.make_async_copy(wk_hbm, wk, wsem.at[2 + 3 * slabs]))
    for copy in loads:
        copy.start()

    barrier = pltpu.get_barrier_semaphore()
    for i in range(1, nreq):
        pl.semaphore_signal(
            barrier, inc=1, device_id=((me + i) % nreq, tp), device_id_type=pl.DeviceIdType.MESH
        )
    for d in range(1, 4):
        pl.semaphore_signal(
            barrier, inc=1, device_id=(me, peer(d)), device_id_type=pl.DeviceIdType.MESH
        )

    spans = []
    at = 0
    while at < width:
        spans.append((at, min(CH, width - at)))
        at += CH

    def blk(r):
        return pl.ds(pl.multiple_of(r * rows, rows), rows)

    loads[0].wait()
    att = att_ref[...]
    for c, (a, w) in enumerate(spans):
        if w < CH:
            psrc[c] = jnp.zeros((rows, CH), BF)
            xs[c] = jnp.zeros((rows, CH), F32)
            gs[c] = jnp.zeros((8, CH), F32)
        psrc[c, :, :w] = lax.dot_general(
            att, wo[a:a + w, :], NT, preferred_element_type=F32
        ).astype(BF)
        xs[c, :, :w] = lin_ref[:, a:a + w].astype(F32)
        gs[c, :, :w] = jnp.broadcast_to(mg_ref[:, a:a + w], (8, w))
    pl.semaphore_wait(barrier, nreq - 1 + 3)
    sends = []
    for d in (2, 3, 1):
        cp = rcopy(psrc.at[peer(d)], prcv.at[d - 1], psnd.at[d - 1], prsem.at[d - 1], me, peer(d))
        cp.start()
        sends.append(cp)
    x1 = xs[tp] + psrc[tp].astype(F32)
    for cp in sends:
        cp.wait()
    for d in range(3):
        x1 = x1 + prcv[d].astype(F32)
    xs[tp] = x1
    lane = lax.broadcasted_iota(jnp.int32, (rows, EX), 1)
    ssq = jnp.sum(x1 * x1, axis=1, keepdims=True)
    high = ssq.astype(BF).astype(F32)
    low = ssq - high
    extra = jnp.where(lane == SSQ0, high, jnp.where(lane == SSQ0 + 1, low, hot_ref[...]))
    yall[tp, blk(me), :CH] = (x1 * gs[tp][:1]).astype(BF)
    yall[tp, blk(me), CH:] = extra.astype(BF)

    sends = []
    for i in range(1, nreq):
        piece = yall.at[tp, blk(me)]
        cp = rcopy(piece, piece, gsnd.at[i], grcv.at[i], (me + i) % nreq, tp)
        cp.start()
        sends.append(cp)
    ty, tc, td = peer(2), peer(1), peer(3)
    for i in range(nreq):
        src = (me + nreq - i) % nreq
        piece = yall.at[tp, blk(src)]
        if i > 0:
            rcopy(piece, piece, gsnd.at[i], grcv.at[i], (me + i) % nreq, tp).wait_recv()
        cp = rcopy(piece, piece, ysnd.at[i], yrcv.at[i], me, ty)
        cp.start()
        sends.append(cp)
        cp = rcopy(piece, piece, csnd.at[0, i], crcv.at[0, i], me, tc)
        cp.start()
        sends.append(cp)
    for i in range(nreq):
        piece = yall.at[ty, blk((me + nreq - i) % nreq)]
        rcopy(piece, piece, ysnd.at[i], yrcv.at[i], me, ty).wait_recv()
        cp = rcopy(piece, piece, csnd.at[1, i], crcv.at[1, i], me, tc)
        cp.start()
        sends.append(cp)
    for i in range(nreq):
        piece = yall.at[tc, blk((me + nreq - i) % nreq)]
        rcopy(piece, piece, csnd.at[0, i], crcv.at[0, i], me, tc).wait_recv()
        piece = yall.at[td, blk((me + nreq - i) % nreq)]
        rcopy(piece, piece, csnd.at[1, i], crcv.at[1, i], me, tc).wait_recv()
    for cp in sends:
        cp.wait_send()

    total = nreq * rows
    lanes = lax.broadcasted_iota(jnp.int32, (total, EX), 1)
    ssq = jnp.zeros((total, 1), F32)
    logits = jnp.zeros((total, EXPERTS), F32)
    for c, (a, w) in enumerate(spans):
        ssq = ssq + jnp.sum(
            jnp.where((lanes >= SSQ0) & (lanes < SSQ0 + 2), yall[c, :, CH:].astype(F32), 0.0), axis=1, keepdims=True
        )
        logits = logits + lax.dot_general(
            yall[c, :, :w], wr_ref[:, a:a + w], NT, preferred_element_type=F32
        )
    scale = lax.rsqrt(ssq / width + EPS)
    logits = logits * scale
    experts = lax.broadcasted_iota(jnp.int32, (total, EXPERTS), 1)
    hot = yall[0, :, CH:CH + EXPERTS].astype(F32) > 0.5
    masked = jnp.where(hot, logits, NEG)
    raw = jnp.where(hot, jnp.exp(masked - jnp.max(masked, axis=1, keepdims=True)), 0.0)
    gates = raw / jnp.sum(raw, axis=1, keepdims=True)

    hidden = []
    for s in range(slabs):
        weight = jnp.sum(
            jnp.where(experts == me * slabs + s, gates, 0.0), axis=1, keepdims=True
        )
        loads[1 + 2 * s].wait()
        loads[2 + 2 * s].wait()
        gate = 0.0
        up = 0.0
        for c, (a, w) in enumerate(spans):
            y = yall[c, :, :w]
            gate = gate + lax.dot_general(y, wg[s, :, a:a + w], NT, preferred_element_type=F32)
            up = up + lax.dot_general(y, wu[s, :, a:a + w], NT, preferred_element_type=F32)
        gate = jnp.minimum(gate * scale, 7.0)
        up = jnp.clip(up * scale, -7.0, 7.0)
        sig = 1.0 / (1.0 + jnp.exp(-1.702 * gate))
        hidden.append(((up + 1.0) * gate * sig * weight).astype(BF))
    for s in range(slabs):
        loads[1 + 2 * slabs + s].wait()
    for c, (a, w) in enumerate(spans):
        acc = 0.0
        for s in range(slabs):
            acc = acc + jnp.dot(hidden[s], wd[s, :, a:a + w], preferred_element_type=F32)
        if w < CH:
            part[c, :, w:] = jnp.zeros((total, CH - w), BF)
        part[c, :, :w] = acc.astype(BF)

    sends = []
    for k, c in ((1, td), (0, tc)):
        cp = rcopy(part.at[c], rb1.at[k], asnd.at[k], arcv.at[k], me, tc)
        cp.start()
        sends.append(cp)
    order = list(range(1, nreq)) + [0]
    sends[0].wait_recv()
    for i in order:
        b = (me + i) % nreq
        sb2[i] = (part[ty, blk(b), :].astype(F32) + rb1[1, blk(b), :].astype(F32)).astype(BF)
        cp = rcopy(sb2.at[i], rb2.at[i], bsnd.at[i], brcv.at[i], me, ty)
        cp.start()
        sends.append(cp)
    sends[1].wait_recv()
    moe = 0.0
    late = []
    for i in order:
        b = (me + i) % nreq
        mine = part[tp, blk(b), :].astype(F32) + rb1[0, blk(b), :].astype(F32)
        rcopy(sb2.at[i], rb2.at[i], bsnd.at[i], brcv.at[i], me, ty).wait_recv()
        mine = mine + rb2[i].astype(F32)
        if i == 0:
            moe = mine
        else:
            sb3[i] = mine.astype(BF)
            cp = rcopy(sb3.at[i], rb3.at[i], dsnd.at[i], drcv.at[i], b, tp)
            cp.start()
            sends.append(cp)
            late.append(cp)
    for n, cp in enumerate(late):
        cp.wait_recv()
        moe = moe + rb3[n + 1].astype(F32)
    x2a[tp] = xs[tp] + moe
    late = []
    for d in (2, 3, 1):
        cp = rcopy(x2a.at[tp], x2a.at[tp], fsnd.at[d - 1], frcv.at[d - 1], me, peer(d))
        cp.start()
        sends.append(cp)
    for d in range(1, 4):
        piece = x2a.at[peer(d)]
        rcopy(piece, piece, fsnd.at[d - 1], frcv.at[d - 1], me, peer(d)).wait_recv()
    for cp in sends:
        cp.wait_send()
    ssq = jnp.zeros((rows, 1), F32)
    for c, (a, w) in enumerate(spans):
        x2 = x2a[c, :, :w]
        lo_ref[:, a:a + w] = x2.astype(BF)
        ssq = ssq + jnp.sum(x2 * x2, axis=1, keepdims=True)
    scale = lax.rsqrt(ssq / width + EPS)
    loads[1 + 3 * slabs].wait()
    loads[2 + 3 * slabs].wait()
    nq = 0.0
    nk = 0.0
    for c, (a, w) in enumerate(spans):
        h3 = (x2a[c, :, :w] * scale * ng_ref[:, a:a + w]).astype(BF)
        nq = nq + jnp.dot(h3, wq[a:a + w, :], preferred_element_type=F32)
        nk = nk + jnp.dot(h3, wk[a:a + w, :], preferred_element_type=F32)
    nq_ref[...] = nq.astype(BF)
    nk_ref[...] = nk.astype(BF)


def tail(att, lin, hot, wo, mg, wr, wg, wu, wd, ng, wq, wk, nreq):
    rows, width = lin.shape
    slabs, ff, _ = wg.shape
    total = nreq * rows
    chunks = -(-width // CH)
    vm = pl.BlockSpec(memory_space=pltpu.VMEM)
    hb = pl.BlockSpec(memory_space=pl.ANY)
    dma = pltpu.SemaphoreType.DMA
    return pl.pallas_call(
        functools.partial(tail_kernel, nreq, slabs, width),
        out_shape=(
            jax.ShapeDtypeStruct((rows, width), BF),
            jax.ShapeDtypeStruct((rows, wq.shape[1]), BF),
            jax.ShapeDtypeStruct((rows, wk.shape[1]), BF),
        ),
        in_specs=[vm, vm, vm, hb, vm, vm, hb, hb, hb, vm, hb, hb],
        out_specs=(vm, vm, vm),
        scratch_shapes=[
            pltpu.VMEM(wo.shape, BF), pltpu.VMEM(wg.shape, BF), pltpu.VMEM(wu.shape, BF),
            pltpu.VMEM(wd.shape, BF), pltpu.VMEM(wq.shape, BF), pltpu.VMEM(wk.shape, BF),
            pltpu.VMEM((chunks, rows, CH), BF),
            pltpu.VMEM((3, rows, CH), BF),
            pltpu.VMEM((chunks, rows, CH), F32),
            pltpu.VMEM((chunks, 8, CH), F32),
            pltpu.VMEM((chunks, total, CH + EX), BF),
            pltpu.VMEM((chunks, total, CH), BF),
            pltpu.VMEM((2, total, CH), BF),
            pltpu.VMEM((nreq, rows, CH), BF),
            pltpu.VMEM((nreq, rows, CH), BF),
            pltpu.VMEM((nreq, rows, CH), BF),
            pltpu.VMEM((nreq, rows, CH), BF),
            pltpu.VMEM((chunks, rows, CH), F32),
            dma((3 + 3 * slabs,)), dma((3,)), dma((3,)), dma((nreq,)), dma((nreq,)),
            dma((nreq,)), dma((nreq,)), dma((2, nreq)), dma((2, nreq)),
            dma((2,)), dma((2,)), dma((nreq,)), dma((nreq,)), dma((nreq,)), dma((nreq,)),
            dma((3,)), dma((3,)),
        ],
        compiler_params=pltpu.CompilerParams(
            collective_id=0, has_side_effects=True, vmem_limit_bytes=58 * 2**20
        ),
        cost_estimate=pl.CostEstimate(
            flops=2 * total * slabs * width * ff * 3, bytes_accessed=33 * 2**20, transcendentals=0
        ),
    )(att, lin, hot, wo, mg, wr, wg, wu, wd, ng, wq, wk)


def swap_kernel(n, spread, count, *refs):
    ins, outs, lands = refs[:count], refs[count:2 * count], refs[2 * count:3 * count]
    ssem, rsem = refs[3 * count:]
    me = lax.axis_index("req")
    tp = lax.axis_index("tp")
    barrier = pltpu.get_barrier_semaphore()
    for i in range(1, n):
        pl.semaphore_signal(
            barrier, inc=1, device_id=((me + i) % n, tp), device_id_type=pl.DeviceIdType.MESH
        )
    pl.semaphore_wait(barrier, n - 1)
    copies = []
    for i in range(1, n):
        to = (me + i) % n
        for a in range(count):
            cp = pltpu.make_async_remote_copy(
                src_ref=ins[a].at[to] if spread else ins[a],
                dst_ref=lands[a].at[me],
                send_sem=ssem.at[a, i],
                recv_sem=rsem.at[a, i],
                device_id=(to, tp),
                device_id_type=pl.DeviceIdType.MESH,
            )
            cp.start()
            copies.append(cp)
    for a in range(count):
        lands[a][me] = ins[a][me] if spread else ins[a][...]
    for cp in copies:
        cp.wait()
    for a in range(count):
        outs[a][...] = lands[a][...]


def swap(arrays, n, spread, ident):
    vm = pl.BlockSpec(memory_space=pltpu.VMEM)
    count = len(arrays)
    shapes = [a.shape if spread else (n,) + a.shape for a in arrays]
    return pl.pallas_call(
        functools.partial(swap_kernel, n, spread, count),
        out_shape=tuple(jax.ShapeDtypeStruct(h, a.dtype) for h, a in zip(shapes, arrays)),
        in_specs=[vm] * count,
        out_specs=(vm,) * count,
        scratch_shapes=[pltpu.VMEM(h, a.dtype) for h, a in zip(shapes, arrays)]
        + [pltpu.SemaphoreType.DMA((count, n)), pltpu.SemaphoreType.DMA((count, n))],
        compiler_params=pltpu.CompilerParams(collective_id=ident, has_side_effects=True),
    )(*arrays)


def local(
    layer_in, query_in, key_in, value_in, prompt_keys, prompt_values, gen_keys, gen_values,
    lengths, parents, routes, sinks, out_weight, mlp_gain, router_weight,
    expert_gate, expert_up, expert_down, next_gain, next_q_weight, next_kv_weight,
):
    req_count = lax.axis_size("req")
    me = lax.axis_index("req")
    T, B, q_width = query_in.shape
    kv_width = key_in.shape[2]
    K = kv_width // HEAD
    R = q_width // kv_width
    J = parents.shape[2]
    span = req_count // J
    beam = me // span
    start = me % span * B
    groups = [[c + span * j for j in range(J)] for c in range(span)]
    if span == 1:
        groups = None
    lens = lax.dynamic_slice_in_dim(lengths, start, B)
    pars = lax.dynamic_slice_in_dim(parents, start, B, axis=1)
    S = prompt_keys.shape[1]
    G = gen_keys.shape[1]
    pos = lens[None, :] + G + jnp.arange(T, dtype=jnp.int32)[:, None]
    q = rope(query_in.astype(F32).reshape(T, B, K * R, HEAD), pos).astype(BF).reshape(T, B, q_width)
    k = rope(key_in.astype(F32).reshape(T, B, K, HEAD), pos).astype(BF).reshape(T, B, kv_width)
    direct = span == 1 and lax.axis_size("tp") == 4
    if direct:
        (q_all,) = swap([q.reshape(T * B, q_width)], J, False, 1)
    else:
        q_all = lax.all_gather(q, "req", axis_index_groups=groups)
    first, tokens = lineage_tables(pars)
    prompt_ok = (beam * S + jnp.arange(S, dtype=jnp.int32))[None, :] < lens[:, None]
    mask = jnp.concatenate(
        [
            jnp.broadcast_to(prompt_ok[:, None, None, :], (B, J, T, S)),
            jnp.broadcast_to((first == beam).transpose(1, 2, 0)[..., None], (B, J, T, G)),
            (tokens == beam).transpose(2, 3, 1, 0),
        ],
        axis=-1,
    )
    keys = jnp.concatenate([prompt_keys, gen_keys, k.transpose(1, 0, 2)], axis=1)
    values = jnp.concatenate([prompt_values, gen_values, value_in.transpose(1, 0, 2)], axis=1)
    keys = keys.reshape(B, S + G + T, K, HEAD)
    values = values.reshape(B, S + G + T, K, HEAD)
    qs = q_all.reshape(J, T, B, K, R, HEAD)
    scores = jnp.einsum("jtbkrd,bskd->bkjtrs", qs, keys, preferred_element_type=F32) * 0.125
    usable = mask[:, None, :, :, None, :]
    scores = jnp.where(usable, scores, NEG)
    high = jnp.max(scores, axis=-1)
    weights = jnp.where(usable, jnp.exp(scores - high[..., None]), 0.0)
    total = jnp.sum(weights, axis=-1)
    part = jnp.einsum("bkjtrs,bskd->jtbkrd", weights.astype(BF), values, preferred_element_type=F32)
    high = high.transpose(2, 3, 0, 1, 4)
    total = total.transpose(2, 3, 0, 1, 4)
    part = (part / jnp.maximum(total, 1e-30)[..., None]).astype(BF)
    stats = jnp.stack([high, total], axis=1)
    if direct:
        form, table = part.shape, stats.shape
        part, stats = swap([part.reshape(J, T * B, q_width), stats.reshape(J, -1, 128)], J, True, 2)
        part, stats = part.reshape(form), stats.reshape(table)
    else:
        part = lax.all_to_all(part, "req", 0, 0, axis_index_groups=groups)
        stats = lax.all_to_all(stats, "req", 0, 0, axis_index_groups=groups)
    high, total = stats[:, 0], stats[:, 1]
    sink = sinks.reshape(K, R)
    peak = jnp.maximum(jnp.max(high, axis=0), sink)
    share = total * jnp.exp(high - peak)
    bottom = jnp.sum(share, axis=0) + jnp.exp(sink - peak)
    attended = jnp.sum(part.astype(F32) * (share / bottom)[..., None], axis=0)
    attended = attended.astype(BF).reshape(T * B, q_width)
    if direct and expert_gate.shape[0] * req_count == EXPERTS:
        hot = jnp.sum(
            (routes.reshape(T * B, -1, 1) == jnp.arange(EX, dtype=jnp.int32)).astype(F32), axis=1
        )
        out, nq, nk = tail(
            attended, layer_in.reshape(T * B, -1), hot, out_weight.T, mlp_gain[None],
            router_weight.T, jnp.swapaxes(expert_gate, 1, 2), jnp.swapaxes(expert_up, 1, 2), expert_down, next_gain[None], next_q_weight,
            next_kv_weight.reshape(-1, 2 * kv_width), req_count,
        )
        return (
            out.reshape(T, B, -1), nq.reshape(T, B, q_width), nk.reshape(T, B, 2, kv_width)
        )
    projected = jnp.dot(attended, out_weight, preferred_element_type=F32)
    x1 = layer_in.reshape(T * B, -1).astype(F32) + lax.psum(projected.astype(BF), "tp").astype(F32)
    h2 = rms(x1, mlp_gain).astype(BF)
    logits = jnp.dot(h2, router_weight, preferred_element_type=F32)
    hot = jnp.sum(
        (routes.reshape(T * B, -1, 1) == jnp.arange(EXPERTS, dtype=jnp.int32)).astype(F32), axis=1
    )
    masked = jnp.where(hot > 0, logits, NEG)
    raw = jnp.where(hot > 0, jnp.exp(masked - jnp.max(masked, axis=-1, keepdims=True)), 0.0)
    gates = raw / jnp.sum(raw, axis=-1, keepdims=True)
    h2_all = lax.all_gather(h2, "req", tiled=True)
    gates_all = lax.all_gather(gates, "req", tiled=True)
    slabs = expert_gate.shape[0]
    split = slabs * req_count // EXPERTS
    moe = 0.0
    for s in range(slabs):
        expert = (me * slabs + s) // split
        weight = lax.dynamic_slice_in_dim(gates_all, expert, 1, axis=1)
        gate = jnp.minimum(jnp.dot(h2_all, expert_gate[s], preferred_element_type=F32), 7.0)
        up = jnp.clip(jnp.dot(h2_all, expert_up[s], preferred_element_type=F32), -7.0, 7.0)
        hidden = ((up + 1.0) * gate * jax.nn.sigmoid(1.702 * gate) * weight).astype(BF)
        moe = moe + jnp.dot(hidden, expert_down[s], preferred_element_type=F32)
    moe = lax.psum_scatter(moe.astype(BF), "req", scatter_dimension=0, tiled=True)
    moe = lax.psum(moe, "tp").astype(F32)
    x2 = x1 + moe
    h3 = rms(x2, next_gain).astype(BF)
    next_query = jnp.dot(h3, next_q_weight, preferred_element_type=F32).astype(BF)
    next_kv = jnp.einsum("nd,dcf->ncf", h3, next_kv_weight, preferred_element_type=F32).astype(BF)
    return (
        x2.astype(BF).reshape(T, B, -1),
        next_query.reshape(T, B, q_width),
        next_kv.reshape(T, B, 2, kv_width),
    )


def solution(mesh):
    placed = (
        P(None, "req", None), P(None, "req", "tp"), P(None, "req", "tp"), P(None, "req", "tp"),
        P("req", None, "tp"), P("req", None, "tp"), P("req", None, "tp"), P("req", None, "tp"),
        P(), P(), P(None, "req", None), P("tp"), P("tp", None), P(), P(),
        P("req", None, "tp"), P("req", None, "tp"), P("req", "tp", None),
        P(), P(None, "tp"), P(None, None, "tp"),
    )
    return jax.shard_map(
        local, mesh=mesh, in_specs=placed,
        out_specs=(P(None, "req", None), P(None, "req", "tp"), P(None, "req", None, "tp")),
        check_vma=False,
    )
```
